128 devices in a mesh: clip: 16 (over y, x), row: 8 (over z, core).
Axes of the slice: x: 4, y: 4, z: 4, core: 2. Of those that a mesh axis runs over, the one named last changes fastest.
Arguments:
- patches: bfloat16 [256, 8, 15360], P(('clip', 'row')), may hold values from -6 to 6
- clip_lengths: int32 [16], replicated, may hold values from 1 to 48, 256 in all
- stem_weight: bfloat16 [48, 192], replicated, may hold values from -0.875 to 0.875
- spatial_weight: bfloat16 [3, 3, 192, 192], replicated, may hold values from -0.15625 to 0.15625
- temporal_weight: bfloat16 [3, 192, 192], replicated, may hold values from -0.25 to 0.25
Outputs:
- block_out: bfloat16 [256, 8, 61440], P(('clip', 'row'))
The draws below stay inside these ranges and needn't reach their ends.
Inputs may be any that keep to these rules, and one draw needn't show every extreme that they name: `clip_lengths`: the 16 clip lengths sum to 256.
All inputs are finite; a program needn't handle non-finite values.
Results may differ from the reference program's by a relative error of at most 0.0055.
Values may be sent and summed in bfloat16 or wider, within the bound.
A program may use at most 64 MiB of HBM per device.

```python
import math
import jax
import jax.numpy as jnp
import numpy as np
from jax import lax

CH = 192
PATCH = 48
COLS = 320
SLAB = 8
LMAX = 48
FRAMES = 256
NCLIPS = 16


def levels(stream_key, extent, split, low, top_value):
    factor_of = 1.0
    for dim, blocks in split:
        steps = jax.random.uniform(jax.random.fold_in(jax.random.fold_in(stream_key, 6), dim), (blocks,), jnp.float32, low / len(split), top_value / len(split))
        factor_of = factor_of * jnp.repeat(jnp.exp(steps), extent[dim] // blocks).reshape((-1,) + (1,) * (len(extent) - 1 - dim))
    return factor_of


def length_profile(count, total, reach, lean):
    loads = [(1 << 20) // math.isqrt(grade ** lean) + 1 for grade in range(2, count + 1)]
    spare, holding = total - reach - (count - 1), [1] * (count - 1)
    while spare > 0:
        free = [i for i in range(count - 1) if holding[i] < reach]
        pool, left = sum([loads[i] for i in free]), spare
        for i in free:
            more = min(reach - holding[i], max(1, left * loads[i] // pool), spare)
            holding[i] = holding[i] + more
            spare = spare - more
    return np.array([reach] + holding)


def ragged(rng, count, total, most, skew):
    if count == 2:
        one = jax.random.randint(rng, (), max(1, total - most), min(most, total - 1) + 1)
        return jnp.stack([one, total - one])
    sizes = jnp.asarray(length_profile(count, total, most, skew), jnp.int32)
    couples = (count - 1) // 2
    donor, receiver = sizes[1:1 + 2 * couples:2], sizes[2:2 + 2 * couples:2]
    margin = jnp.minimum(donor - 1, most - receiver)
    shifted = jax.random.randint(jax.random.fold_in(rng, 1), (couples,), 0, 1 << 20) % (margin + 1)
    sizes = sizes.at[1:1 + 2 * couples:2].set(donor - shifted).at[2:2 + 2 * couples:2].set(receiver + shifted)
    return sizes[jax.random.permutation(jax.random.fold_in(rng, 2), count)]


def gaussian(key, extent, scale, limit, shards=(), held_as=jnp.bfloat16):
    level = levels(key, extent, shards, -0.22, 0.18) if shards else 1.0
    array = jax.random.normal(key, extent, jnp.float32) * scale * level
    return jnp.minimum(jnp.maximum(array, -limit), limit).astype(held_as)


def setup_inputs(seed: int = 0) -> dict:
    seeds = jax.random.split(jax.random.key(seed), 6)
    return {
        "patches": gaussian(seeds[0], (FRAMES, SLAB, COLS * PATCH), 1.0, 6.0, ((0, 128),)),
        "clip_lengths": ragged(seeds[1], NCLIPS, FRAMES, LMAX, 2).astype(jnp.int32),
        "stem_weight": gaussian(seeds[2], (PATCH, CH), PATCH ** -0.5, 0.875),
        "spatial_weight": gaussian(seeds[3], (3, 3, CH, CH), (9 * CH) ** -0.5, 0.15625),
        "temporal_weight": gaussian(seeds[4], (3, CH, CH), (3 * CH) ** -0.5, 0.25),
    }


def find_starts(clip_lengths, frame_ids):
    clip_ends = jnp.cumsum(clip_lengths).astype(jnp.int32)
    clip_firsts = (clip_ends - clip_lengths).astype(jnp.int32)
    inside = clip_firsts[None, :] <= frame_ids[:, None]
    return jnp.max(jnp.where(inside, clip_firsts[None, :], 0), axis=1).astype(jnp.int32)


def reference(patches, clip_lengths, stem_weight, spatial_weight, temporal_weight):
    blocks = FRAMES // 16

    def front_part(frame_block):
        pieces = frame_block.reshape(16, SLAB, COLS, PATCH).astype(jnp.float32)
        features = jnp.einsum('fhwp,pc->fhwc', pieces, stem_weight.astype(jnp.float32)).astype(jnp.bfloat16)
        padded = jnp.pad(features.astype(jnp.float32), ((0, 0), (1, 1), (1, 1), (0, 0)))
        summed = jnp.zeros((16, SLAB, COLS, CH), jnp.float32)
        for row_shift in range(3):
            for col_shift in range(3):
                window = padded[:, row_shift:row_shift + SLAB, col_shift:col_shift + COLS, :]
                summed = summed + jnp.einsum('fhwc,cd->fhwd', window, spatial_weight[row_shift, col_shift].astype(jnp.float32))
        return features, summed.astype(jnp.bfloat16)

    features, spatial = lax.map(front_part, patches.reshape(blocks, 16, SLAB, COLS * PATCH))
    features = features.reshape(FRAMES, SLAB, COLS, CH)
    spatial = spatial.reshape(FRAMES, SLAB, COLS, CH)
    frame_ids = jnp.arange(FRAMES, dtype=jnp.int32)
    clip_start = find_starts(clip_lengths, frame_ids)

    def back_part(inputs):
        block_ids, block_first = inputs
        summed = jnp.zeros((16, SLAB, COLS, CH), jnp.float32)
        for lag_step in range(3):
            source = jnp.maximum(block_ids - lag_step, block_first).astype(jnp.int32)
            taken = jnp.take(spatial, source, axis=0).astype(jnp.float32)
            summed = summed + jnp.einsum('fhwc,cd->fhwd', taken, temporal_weight[lag_step].astype(jnp.float32))
        branch = jax.nn.silu(summed).astype(jnp.bfloat16)
        branch = lax.optimization_barrier(branch)
        own = jnp.take(features, block_ids, axis=0).astype(jnp.float32)
        return (own + branch.astype(jnp.float32)).astype(jnp.bfloat16)

    result = lax.map(back_part, (frame_ids.reshape(blocks, 16), clip_start.reshape(blocks, 16)))
    return result.reshape(FRAMES, SLAB, COLS * CH)
```

```python
import jax
import jax.numpy as jnp
from jax import lax
from jax.experimental import pallas as pl
from jax.experimental.pallas import tpu as pltpu
from jax.sharding import PartitionSpec as P

MESH = pl.DeviceIdType.MESH
BF16, F32 = jnp.bfloat16, jnp.float32

CH = 192
PATCH = 48
COLS = 320
SLAB = 8
LANES = COLS * PATCH
PAIRS = 20
TILES = 6
HALF = 320
CHUNKS = 2
LAST = 127
READS = ((0, 3), (0, 1), (0, 1), (1, 2), (1, 2), (2, 4))


def lane_block(tile, block):
    if tile == 0:
        return block if block < 12 else block - 16
    if tile == 5:
        return block + 16 if block < 12 else block
    return block if tile < 3 else block + 8


def mix(a, b):
    return jnp.dot(a, b, preferred_element_type=F32)


def spread(values, keep, kind):
    rows = values.shape[0]
    wide = jnp.concatenate([values, jnp.zeros((rows, 64), F32)], axis=1)
    back = pltpu.roll(wide, 192, 1)
    ahead = pltpu.roll(wide, 64, 1)
    keep[kind + (0,)] = wide[:, :128].astype(BF16)
    keep[kind + (1,)] = back[:, :128].astype(BF16)
    keep[kind + (2,)] = wide[:, 128:].astype(BF16)
    keep[kind + (3,)] = ahead[:, :128].astype(BF16)


def block_of(small, tile, half, block, base, first, count):
    lanes = 2 * tile + half
    pixel = 2 * (lanes // 3)
    place = lane_block(tile, block)

    def take(pix, arrangement):
        row = place - 3 * (pix + first)
        if 0 <= row < count:
            return small(arrangement, base + 16 * row)
        return None

    if lanes % 3 == 0:
        parts = [take(pixel, 0)]
    elif lanes % 3 == 2:
        parts = [take(pixel + 1, 1)]
    else:
        parts = [take(pixel, 2), take(pixel + 1, 3)]
    parts = [part for part in parts if part is not None]
    if not parts:
        return jnp.zeros((16, 128), BF16)
    return parts[0] if len(parts) == 1 else parts[0] + parts[1]


def kernel(
    lengths, patches, stem_hbm, spatial_hbm, temporal_hbm, out,
    own, halo, stem, spatial, temporal, folded, small, small_stem, wide, wide_stem, rows, acc, feats,
    load_sem, send_sem, recv_sem,
):
    clip, row = lax.axis_index("clip"), lax.axis_index("row")
    me = clip * 8 + row

    def place(device):
        return (device // 8, lax.rem(device, 8))

    loads = [
        pltpu.make_async_copy(spatial_hbm, spatial, load_sem.at[0]),
        pltpu.make_async_copy(stem_hbm, stem, load_sem.at[1]),
        pltpu.make_async_copy(temporal_hbm, temporal, load_sem.at[2]),
        pltpu.make_async_copy(patches, own.at[:, :, pl.ds(128, LANES)], load_sem.at[3]),
    ]
    barrier = pltpu.get_barrier_semaphore()

    @pl.when(me > 0)
    def _():
        pl.semaphore_signal(barrier, inc=1, device_id=place(me - 1), device_id_type=MESH)

    for load in loads:
        load.start()

    cuts = [PAIRS * c // CHUNKS for c in range(CHUNKS + 1)]
    edges = [0] + [768 * cut + 128 for cut in cuts[1:-1]] + [LANES]
    sends = [
        pltpu.make_async_remote_copy(
            patches.at[:, :, pl.ds(lo, hi - lo)],
            halo.at[:, :, pl.ds(128 + lo, hi - lo)],
            send_sem.at[c],
            recv_sem.at[c],
            device_id=place(jnp.minimum(me + 1, LAST)),
            device_id_type=MESH,
        )
        for c, (lo, hi) in enumerate(zip(edges[:-1], edges[1:]))
    ]

    @pl.when(me < LAST)
    def _():
        pl.semaphore_wait(barrier, 1)
        for send in sends:
            send.start()

    first, total = jnp.int32(0), jnp.int32(0)
    first_next = jnp.int32(0)
    for k in range(16):
        first = jnp.where(total <= 2 * me, total, first)
        first_next = jnp.where(total <= 2 * me + 1, total, first_next)
        total = total + lengths[k]
    room0 = 2 * me - first
    room1 = 2 * me + 1 - first_next

    side = jnp.zeros((2, SLAB, 128), BF16)
    for ref in (own, halo):
        ref[:, :, :128] = side
        ref[:, :, LANES + 128:] = side

    loads[0].wait()
    loads[1].wait()
    for tap in range(9):
        folded[48 * tap : 48 * tap + 48] = mix(stem[...], spatial[tap // 3, tap % 3])
    spread(stem[...].astype(F32), small_stem, ())
    loads[2].wait()
    upper = folded[...].astype(BF16)
    lower = (folded[...] - upper.astype(F32)).astype(BF16)
    for t in range(3):
        spread(mix(upper, temporal[t]) + mix(lower, temporal[t]), small, (t,))

    def widen(tap, carry):
        t, a = tap // 3, lax.rem(tap, 3)
        base = a * 144
        for tile in range(TILES):
            for half in range(2):
                for block in range(16):
                    value = block_of(
                        lambda arrangement, row: small[t, arrangement, pl.ds(pl.multiple_of(row, 16), 16)],
                        tile, half, block, base, -1, 9,
                    )
                    where = pl.ds(pl.multiple_of(tap * 256 + 16 * block, 16), 16)
                    wide[tile, where, 128 * half : 128 * half + 128] = value
        return carry

    lax.fori_loop(0, 9, widen, 0)
    for tile in range(TILES):
        for half in range(2):
            for block in range(16):
                wide_stem[tile, 16 * block : 16 * block + 16, 128 * half : 128 * half + 128] = block_of(
                    lambda arrangement, row: small_stem[arrangement, row : row + 16], tile, half, block, 0, 0, 3
                )

    band = lax.broadcasted_iota(jnp.int32, (SLAB, 1024), 0)
    lane = lax.broadcasted_iota(jnp.int32, (SLAB, 128), 1)

    def put(source, t, frame, pair):
        shifted = (
            jnp.where(band == 0, 0.0, pltpu.roll(source, 1, 0)),
            source,
            jnp.where(band == SLAB - 1, 0.0, pltpu.roll(source, SLAB - 1, 0)),
        )
        where = pl.ds(pl.multiple_of(frame * HALF + pair * 16, 16), 16)
        for a, values in enumerate(shifted):
            groups = []
            for at in (0, 384):
                tiles = [values[:, at + 128 * i : at + 128 * i + 128] for i in range(5)]
                groups.append(
                    (tiles[1], tiles[2], tiles[3],
                     jnp.where(lane < 64, tiles[2], tiles[0]), jnp.where(lane < 64, tiles[4], tiles[2]))
                )
            for i in range(5):
                both = jnp.concatenate([groups[0][i], groups[1][i]], axis=0)
                rows[t, a, i, where] = both.astype(BF16)

    def lanes_of(ref, frame, pair):
        return ref[frame, :, pl.ds(pl.multiple_of(pair * 768, 128), 1024)].astype(F32)

    loads[3].wait()

    def own_rows(pair, carry):
        own0, own1 = lanes_of(own, 0, pair), lanes_of(own, 1, pair)
        put(own0, 0, 0, pair)
        put(own1, 0, 1, pair)
        put(jnp.where(room1 >= 1, own0, own1), 1, 1, pair)
        return carry

    lax.fori_loop(0, PAIRS, own_rows, 0)

    def left_side(t, tile, lo, count):
        i, j = READS[tile]
        return jnp.concatenate(
            [rows[t, a, k, lo : lo + count] for a in range(3) for k in (i, j)], axis=1
        )

    for tile in range(TILES):
        i, j = READS[tile]
        centre = jnp.concatenate([rows[0, 1, i], rows[0, 1, j]], axis=1)
        feats[tile] = mix(centre, wide_stem[tile]).astype(BF16)
        acc[tile] = mix(left_side(0, tile, 0, 2 * HALF), wide[tile, 0:768])
        acc[tile, HALF:] += mix(left_side(1, tile, HALF, HALF), wide[tile, 768:1536])

    def halo_rows(pair, carry):
        own0, own1 = lanes_of(own, 0, pair), lanes_of(own, 1, pair)
        halo0, halo1 = lanes_of(halo, 0, pair), lanes_of(halo, 1, pair)
        tap01 = jnp.where(room0 >= 1, halo1, own0)
        put(tap01, 1, 0, pair)
        put(jnp.where(room0 >= 2, halo0, tap01), 2, 0, pair)
        tap11 = jnp.where(room1 >= 1, own0, own1)
        put(jnp.where(room1 >= 2, halo1, tap11), 2, 1, pair)
        return carry

    for c in range(CHUNKS):
        @pl.when(me > 0)
        def _():
            sends[c].wait_recv()

        lax.fori_loop(cuts[c], cuts[c + 1], halo_rows, 0)
        lo, count = 16 * cuts[c], 16 * (cuts[c + 1] - cuts[c])
        for tile in range(TILES):
            tap1 = mix(left_side(1, tile, lo, count), wide[tile, 768:1536])
            for frame in range(2):
                at = frame * HALF + lo
                value = acc[tile, at : at + count] + mix(left_side(2, tile, at, count), wide[tile, 1536:])
                if frame == 0:
                    value = value + tap1
                branch = (value * (0.5 * jnp.tanh(0.5 * value) + 0.5)).astype(BF16)
                result = (feats[tile, at : at + count].astype(F32) + branch.astype(F32)).astype(BF16)
                for g in range(count // 8):
                    to = (lo // 8 + g) * 1536 + 256 * tile
                    out[frame, :, to : to + 256] = result[8 * g : 8 * g + 8]

    @pl.when(me < LAST)
    def _():
        for send in sends:
            send.wait_send()


def body(patches, clip_lengths, stem_weight, spatial_weight, temporal_weight):
    hbm = pl.BlockSpec(memory_space=pltpu.HBM)
    return pl.pallas_call(
        kernel,
        out_shape=pltpu.VMEM((2, SLAB, COLS * CH), BF16),
        in_specs=[pl.BlockSpec(memory_space=pltpu.SMEM), hbm, hbm, hbm, hbm],
        scratch_shapes=[
            pltpu.VMEM((2, SLAB, LANES + 256), BF16),
            pltpu.VMEM((2, SLAB, LANES + 256), BF16),
            pltpu.VMEM((PATCH, CH), BF16),
            pltpu.VMEM((3, 3, CH, CH), BF16),
            pltpu.VMEM((3, CH, CH), BF16),
            pltpu.VMEM((9 * PATCH, CH), F32),
            pltpu.VMEM((3, 4, 9 * PATCH, 128), BF16),
            pltpu.VMEM((4, PATCH, 128), BF16),
            pltpu.VMEM((TILES, 9 * 256, 256), BF16),
            pltpu.VMEM((TILES, 256, 256), BF16),
            pltpu.VMEM((3, 3, 5, 2 * HALF, 128), BF16),
            pltpu.VMEM((TILES, 2 * HALF, 256), F32),
            pltpu.VMEM((TILES, 2 * HALF, 256), BF16),
            pltpu.SemaphoreType.DMA((4,)),
            pltpu.SemaphoreType.DMA((CHUNKS,)),
            pltpu.SemaphoreType.DMA((CHUNKS,)),
        ],
        compiler_params=pltpu.CompilerParams(
            collective_id=0, has_side_effects=True, vmem_limit_bytes=44 << 20
        ),
        cost_estimate=pl.CostEstimate(flops=10_000_000_000, bytes_accessed=4_000_000, transcendentals=1_000_000),
    )(clip_lengths, patches, stem_weight, spatial_weight, temporal_weight)


def solution(mesh):
    return jax.shard_map(
        body,
        mesh=mesh,
        in_specs=(P(("clip", "row"), None, None), P(), P(), P(), P()),
        out_specs=P(("clip", "row"), None, None),
        check_vma=False,
    )
```

```python
import jax
import jax.numpy as jnp
from jax import lax
from jax.experimental import pallas as pl
from jax.experimental.pallas import tpu as pltpu
from jax.sharding import PartitionSpec as P

MESH = pl.DeviceIdType.MESH
BF16, F32 = jnp.bfloat16, jnp.float32

CH = 192
PATCH = 48
COLS = 320
SLAB = 8
LANES = COLS * PATCH
GROUPS = 40
TILES = 3
HALF = 640
CUTS = (0, 10, 20, 30, 40)
CHUNKS = len(CUTS) - 1
LAST = 127
STEP = 160
READS = ((0, 2), (0, 1), (0, 1))


def lane_block(tile, block):
    return block - 16 if tile == 0 and block >= 12 else block


def mix(a, b):
    return jnp.dot(a, b, preferred_element_type=F32)


def spread(values, keep, kind):
    rows = values.shape[0]
    wide = jnp.concatenate([values, jnp.zeros((rows, 64), F32)], axis=1)
    back = pltpu.roll(wide, 192, 1)
    ahead = pltpu.roll(wide, 64, 1)
    keep[kind + (0,)] = wide[:, :128].astype(BF16)
    keep[kind + (1,)] = back[:, :128].astype(BF16)
    keep[kind + (2,)] = wide[:, 128:].astype(BF16)
    keep[kind + (3,)] = ahead[:, :128].astype(BF16)


def block_of(small, tile, half, block, base, first, count):
    lanes = 2 * tile + half
    pixel = 2 * (lanes // 3)
    place = lane_block(tile, block)

    def take(pix, arrangement):
        row = place - 3 * (pix + first)
        if 0 <= row < count:
            return small(arrangement, base + 16 * row)
        return None

    if lanes % 3 == 0:
        parts = [take(pixel, 0)]
    elif lanes % 3 == 2:
        parts = [take(pixel + 1, 1)]
    else:
        parts = [take(pixel, 2), take(pixel + 1, 3)]
    parts = [part for part in parts if part is not None]
    if not parts:
        return jnp.zeros((16, 128), BF16)
    return parts[0] if len(parts) == 1 else parts[0] + parts[1]


def kernel(
    lengths_hbm, patches, stem_hbm, spatial_hbm, temporal_hbm, out,
    lengths, own, halo, stem, spatial, temporal, folded, small, small_stem, wide, wide_stem, rows, acc, feats,
    load_sem, send_sem, recv_sem,
):
    clip, row = lax.axis_index("clip"), lax.axis_index("row")
    me = clip * 8 + row

    def place(device):
        return (device // 8, lax.rem(device, 8))

    loads = [
        pltpu.make_async_copy(spatial_hbm, spatial, load_sem.at[0]),
        pltpu.make_async_copy(stem_hbm, stem, load_sem.at[1]),
        pltpu.make_async_copy(temporal_hbm, temporal, load_sem.at[2]),
        pltpu.make_async_copy(patches, own.at[:, :, pl.ds(128, LANES)], load_sem.at[3]),
        pltpu.make_async_copy(lengths_hbm, lengths, load_sem.at[4]),
    ]
    barrier = pltpu.get_barrier_semaphore()

    @pl.when(me > 0)
    def _():
        pl.semaphore_signal(barrier, inc=1, device_id=place(me - 1), device_id_type=MESH)

    cuts = CUTS
    edges = [0] + [384 * cut + 128 for cut in cuts[1:-1]] + [LANES]
    sends = [
        pltpu.make_async_remote_copy(
            patches.at[:, :, pl.ds(lo, hi - lo)],
            halo.at[:, :, pl.ds(128 + lo, hi - lo)],
            send_sem.at[c],
            recv_sem.at[c],
            device_id=place(jnp.minimum(me + 1, LAST)),
            device_id_type=MESH,
        )
        for c, (lo, hi) in enumerate(zip(edges[:-1], edges[1:]))
    ]

    def start_sends():
        pl.semaphore_wait(barrier, 1)
        for send in sends:
            send.start()

    ends = row >= 6
    pl.when(jnp.logical_and(ends, me < LAST))(start_sends)
    for load in loads:
        load.start()

    loads[4].wait()
    first, total = jnp.int32(0), jnp.int32(0)
    first_next = jnp.int32(0)
    for k in range(16):
        first = jnp.where(total <= 2 * me, total, first)
        first_next = jnp.where(total <= 2 * me + 1, total, first_next)
        total = total + lengths[k]
    room0 = 2 * me - first
    room1 = 2 * me + 1 - first_next

    side = jnp.zeros((2, SLAB, 128), BF16)
    for ref in (own, halo):
        ref[:, :, :128] = side
        ref[:, :, LANES + 128:] = side

    loads[0].wait()
    loads[1].wait()
    for tap in range(9):
        folded[48 * tap : 48 * tap + 48] = mix(stem[...], spatial[tap // 3, tap % 3])
    spread(stem[...].astype(F32), small_stem, ())
    pl.when(jnp.logical_not(ends))(start_sends)
    loads[2].wait()
    upper = folded[...].astype(BF16)
    lower = (folded[...] - upper.astype(F32)).astype(BF16)
    for t in range(3):
        spread(mix(upper, temporal[t]) + mix(lower, temporal[t]), small, (t,))

    def widen(tap, carry):
        t, a = tap // 3, lax.rem(tap, 3)
        base = a * 144
        for tile in range(TILES):
            for half in range(2):
                for block in range(16):
                    value = block_of(
                        lambda arrangement, row: small[t, arrangement, pl.ds(pl.multiple_of(row, 16), 16)],
                        tile, half, block, base, -1, 9,
                    )
                    where = pl.ds(pl.multiple_of(tap * 256 + 16 * block, 16), 16)
                    wide[tile, where, 128 * half : 128 * half + 128] = value
        return carry

    lax.fori_loop(0, 9, widen, 0)
    for tile in range(TILES):
        for half in range(2):
            for block in range(16):
                wide_stem[tile, 16 * block : 16 * block + 16, 128 * half : 128 * half + 128] = block_of(
                    lambda arrangement, row: small_stem[arrangement, row : row + 16], tile, half, block, 0, 0, 3
                )

    band = lax.broadcasted_iota(jnp.int32, (SLAB, 128), 0)
    left = lax.broadcasted_iota(jnp.int32, (SLAB, 128), 1) < 64

    def put(source, t, frame, group):
        tiles = [source[:, 128 * i : 128 * i + 128] for i in range(5)]
        turned = [pltpu.roll(tiles[i], 64, 1) for i in (2, 3, 4)]
        even = (tiles[1], tiles[2], jnp.where(left, tiles[2], tiles[0]))
        odd = (
            jnp.where(left, turned[0], turned[1]),
            jnp.where(left, turned[1], turned[2]),
            jnp.where(left, turned[1], turned[0]),
        )
        where = pl.ds(pl.multiple_of(frame * HALF + group * 16, 16), 16)
        for k in range(3):
            down = [jnp.where(band == 0, 0.0, pltpu.roll(x[k], 1, 0)) for x in (even, odd)]
            up = [jnp.where(band == SLAB - 1, 0.0, pltpu.roll(x[k], SLAB - 1, 0)) for x in (even, odd)]
            for a, both in enumerate((down, [even[k], odd[k]], up)):
                rows[t, a, k, where] = jnp.concatenate(both, axis=0).astype(BF16)

    def lanes_of(ref, frame, group):
        return ref[frame, :, pl.ds(pl.multiple_of(group * 384, 128), 640)].astype(F32)

    loads[3].wait()

    def own_rows(group, carry):
        own0, own1 = lanes_of(own, 0, group), lanes_of(own, 1, group)
        put(own0, 0, 0, group)
        put(own1, 0, 1, group)
        put(jnp.where(room1 >= 1, own0, own1), 1, 1, group)
        return carry

    lax.fori_loop(0, GROUPS, own_rows, 0, unroll=10)

    def left_side(t, tile, lo, count):
        return jnp.concatenate(
            [rows[t, a, k, lo : lo + count] for a in range(3) for k in READS[tile]], axis=1
        )

    for tile in range(TILES):
        centre = jnp.concatenate([rows[0, 1, k] for k in READS[tile]], axis=1)
        feats[tile] = mix(centre, wide_stem[tile]).astype(BF16)
        for at in range(0, HALF, STEP):
            acc[tile, at : at + STEP] = mix(left_side(0, tile, at, STEP), wide[tile, 0:768])
        for at in range(HALF, 2 * HALF, STEP):
            both = jnp.concatenate([left_side(0, tile, at, STEP), left_side(1, tile, at, STEP)], axis=1)
            acc[tile, at : at + STEP] = mix(both, wide[tile, 0:1536])

    def halo_rows(group, carry):
        own0, own1 = lanes_of(own, 0, group), lanes_of(own, 1, group)
        halo0, halo1 = lanes_of(halo, 0, group), lanes_of(halo, 1, group)
        tap01 = jnp.where(room0 >= 1, halo1, own0)
        put(tap01, 1, 0, group)
        put(jnp.where(room0 >= 2, halo0, tap01), 2, 0, group)
        tap11 = jnp.where(room1 >= 1, own0, own1)
        put(jnp.where(room1 >= 2, halo1, tap11), 2, 1, group)
        return carry

    for c in range(CHUNKS):
        @pl.when(me > 0)
        def _():
            sends[c].wait_recv()

        lax.fori_loop(cuts[c], cuts[c + 1], halo_rows, 0, unroll=10)
        lo, count = 16 * cuts[c], 16 * (cuts[c + 1] - cuts[c])
        for tile in range(TILES):
            tap1 = mix(left_side(1, tile, lo, count), wide[tile, 768:1536])
            sides = [left_side(2, tile, lo + at, count) for at in (0, HALF)]
            tap2 = mix(jnp.concatenate(sides, axis=0), wide[tile, 1536:])
            for frame in range(2):
                at = frame * HALF + lo
                value = acc[tile, at : at + count] + tap2[frame * count : (frame + 1) * count]
                if frame == 0:
                    value = value + tap1
                branch = (value * (0.5 * jnp.tanh(0.5 * value) + 0.5)).astype(BF16)
                result = (feats[tile, at : at + count].astype(F32) + branch.astype(F32)).astype(BF16)
                for g in range(count // 8):
                    to = (lo // 8 + g) * 768 + 256 * tile
                    out[frame, :, to : to + 256] = result[8 * g : 8 * g + 8]

    @pl.when(me < LAST)
    def _():
        for send in sends:
            send.wait_send()


def body(patches, clip_lengths, stem_weight, spatial_weight, temporal_weight):
    operands = (clip_lengths, patches, stem_weight, spatial_weight, temporal_weight)
    return pl.pallas_call(
        kernel,
        out_shape=pltpu.VMEM((2, SLAB, COLS * CH), BF16),
        in_specs=[pl.BlockSpec(memory_space=pltpu.HBM)] * 5,
        scratch_shapes=[
            pltpu.SMEM((16,), jnp.int32),
            pltpu.VMEM((2, SLAB, LANES + 256), BF16),
            pltpu.VMEM((2, SLAB, LANES + 256), BF16),
            pltpu.VMEM((PATCH, CH), BF16),
            pltpu.VMEM((3, 3, CH, CH), BF16),
            pltpu.VMEM((3, CH, CH), BF16),
            pltpu.VMEM((9 * PATCH, CH), F32),
            pltpu.VMEM((3, 4, 9 * PATCH, 128), BF16),
            pltpu.VMEM((4, PATCH, 128), BF16),
            pltpu.VMEM((TILES, 9 * 256, 256), BF16),
            pltpu.VMEM((TILES, 256, 256), BF16),
            pltpu.VMEM((3, 3, 3, 2 * HALF, 128), BF16),
            pltpu.VMEM((TILES, 2 * HALF, 256), F32),
            pltpu.VMEM((TILES, 2 * HALF, 256), BF16),
            pltpu.SemaphoreType.DMA((5,)),
            pltpu.SemaphoreType.DMA((CHUNKS,)),
            pltpu.SemaphoreType.DMA((CHUNKS,)),
        ],
        compiler_params=pltpu.CompilerParams(
            collective_id=0, has_side_effects=True, vmem_limit_bytes=44 << 20
        ),
        cost_estimate=pl.CostEstimate(flops=10_000_000_000, bytes_accessed=4_000_000, transcendentals=1_000_000),
    )(*[pltpu.with_memory_space_constraint(x, pltpu.HBM) for x in operands])


def solution(mesh):
    return jax.shard_map(
        body,
        mesh=mesh,
        in_specs=(P(("clip", "row"), None, None), P(), P(), P(), P()),
        out_specs=P(("clip", "row"), None, None),
        check_vma=False,
    )
```

```python
import functools

import jax
import jax.numpy as jnp
from jax import lax
from jax.experimental import pallas as pl
from jax.experimental.pallas import tpu as pltpu
from jax.sharding import PartitionSpec as P

MESH = pl.DeviceIdType.MESH
BF16, F32 = jnp.bfloat16, jnp.float32

CH = 192
PATCH = 48
COLS = 320
SLAB = 8
LANES = COLS * PATCH
GROUPS = 40
TILES = 3
HALF = 640
CUTS1 = (0, 14, 28, 40)
CUTS0 = (0, 14, 28, 40)
CHUNKS = len(CUTS1) + len(CUTS0) - 2
LAST = 127
STEP = 160
SPANS = ((0, 256, (0, 2)), (256, 768, (0, 1)))


def lane_block(tile, block):
    return block - 16 if tile == 0 and block >= 12 else block


def mix(a, b):
    return jnp.dot(a, b, preferred_element_type=F32)


def spread(values, keep, kind):
    rows = values.shape[0]
    wide = jnp.concatenate([values, jnp.zeros((rows, 64), F32)], axis=1)
    back = pltpu.roll(wide, 192, 1)
    ahead = pltpu.roll(wide, 64, 1)
    keep[kind + (0,)] = wide[:, :128].astype(BF16)
    keep[kind + (1,)] = back[:, :128].astype(BF16)
    keep[kind + (2,)] = wide[:, 128:].astype(BF16)
    keep[kind + (3,)] = ahead[:, :128].astype(BF16)


def block_of(small, tile, half, block, base, first, count):
    lanes = 2 * tile + half
    pixel = 2 * (lanes // 3)
    place = lane_block(tile, block)

    def take(pix, arrangement):
        row = place - 3 * (pix + first)
        if 0 <= row < count:
            return small(arrangement, base + 16 * row)
        return None

    if lanes % 3 == 0:
        parts = [take(pixel, 0)]
    elif lanes % 3 == 2:
        parts = [take(pixel + 1, 1)]
    else:
        parts = [take(pixel, 2), take(pixel + 1, 3)]
    parts = [part for part in parts if part is not None]
    if not parts:
        return None
    return parts[0] if len(parts) == 1 else parts[0] + parts[1]


def kernel(
    lengths_hbm, patches, stem_hbm, spatial_hbm, temporal_hbm, out,
    lengths, own, halo, stem, spatial, temporal, folded, small, small_stem, wide, wide_stem, rows, acc, feats,
    load_sem, send_sem, recv_sem,
):
    clip, row = lax.axis_index("clip"), lax.axis_index("row")
    me = clip * 8 + row

    def place(device):
        return (device // 8, lax.rem(device, 8))

    loads = [
        pltpu.make_async_copy(spatial_hbm, spatial, load_sem.at[0]),
        pltpu.make_async_copy(stem_hbm, stem, load_sem.at[1]),
        pltpu.make_async_copy(temporal_hbm, temporal, load_sem.at[2]),
        pltpu.make_async_copy(patches, own.at[:, :, pl.ds(128, LANES)], load_sem.at[3]),
        pltpu.make_async_copy(lengths_hbm, lengths, load_sem.at[4]),
    ]
    barrier = pltpu.get_barrier_semaphore()

    @pl.when(me > 0)
    def _():
        pl.semaphore_signal(barrier, inc=1, device_id=place(me - 1), device_id_type=MESH)

    sends, pieces = [], []
    for frame, cuts in ((1, CUTS1), (0, CUTS0)):
        edges = [0] + [384 * cut + 128 for cut in cuts[1:-1]] + [LANES]
        for c in range(len(cuts) - 1):
            lo, hi = edges[c], edges[c + 1]
            pieces.append((frame, cuts[c], cuts[c + 1]))
            sends.append(
                pltpu.make_async_remote_copy(
                    patches.at[frame, :, pl.ds(lo, hi - lo)],
                    halo.at[frame, :, pl.ds(128 + lo, hi - lo)],
                    send_sem.at[len(sends)],
                    recv_sem.at[len(sends)],
                    device_id=place(jnp.minimum(me + 1, LAST)),
                    device_id_type=MESH,
                )
            )

    def start_sends():
        pl.semaphore_wait(barrier, 1)
        for send in sends:
            send.start()

    ends = row >= 6
    pl.when(jnp.logical_and(ends, me < LAST))(start_sends)
    for load in loads:
        load.start()

    loads[4].wait()
    first, total = jnp.int32(0), jnp.int32(0)
    first_next = jnp.int32(0)
    for k in range(16):
        first = jnp.where(total <= 2 * me, total, first)
        first_next = jnp.where(total <= 2 * me + 1, total, first_next)
        total = total + lengths[k]
    room0 = 2 * me - first
    room1 = 2 * me + 1 - first_next

    side = jnp.zeros((2, SLAB, 128), BF16)
    for ref in (own, halo):
        ref[:, :, :128] = side
        ref[:, :, LANES + 128:] = side

    def clear(tap, carry):
        for tile in range(TILES):
            for half in range(2):
                for block in range(16):
                    if block_of(lambda arrangement, row: 0, tile, half, block, 0, -1, 9) is None:
                        to = pl.ds(pl.multiple_of(tap * 256 + 16 * block, 16), 16)
                        lanes = 256 * tile + 128 * half
                        wide[to, lanes : lanes + 128] = jnp.zeros((16, 128), BF16)
        return carry

    lax.fori_loop(0, 9, clear, 0)
    loads[0].wait()
    loads[1].wait()
    for tap in range(9):
        folded[48 * tap : 48 * tap + 48] = mix(stem[...], spatial[tap // 3, tap % 3])
    spread(stem[...].astype(F32), small_stem, ())
    loads[2].wait()
    upper = folded[...].astype(BF16)
    lower = (folded[...] - upper.astype(F32)).astype(BF16)
    for t in range(3):
        spread(mix(upper, temporal[t]) + mix(lower, temporal[t]), small, (t,))

    def widen(tap, carry):
        t, a = tap // 3, lax.rem(tap, 3)
        base = a * 144
        for tile in range(TILES):
            for half in range(2):
                for block in range(16):
                    value = block_of(
                        lambda arrangement, row: small[t, arrangement, pl.ds(pl.multiple_of(row, 16), 16)],
                        tile, half, block, base, -1, 9,
                    )
                    to = pl.ds(pl.multiple_of(tap * 256 + 16 * block, 16), 16)
                    lanes = 256 * tile + 128 * half
                    if value is not None:
                        wide[to, lanes : lanes + 128] = value
        return carry

    lax.fori_loop(0, 9, widen, 0)
    for tile in range(TILES):
        for half in range(2):
            for block in range(16):
                value = block_of(
                    lambda arrangement, row: small_stem[arrangement, row : row + 16], tile, half, block, 0, 0, 3
                )
                lanes = 256 * tile + 128 * half
                wide_stem[16 * block : 16 * block + 16, lanes : lanes + 128] = (
                    jnp.zeros((16, 128), BF16) if value is None else value
                )

    pl.when(jnp.logical_not(ends))(start_sends)

    band = lax.broadcasted_iota(jnp.int32, (SLAB, 128), 0)
    left = lax.broadcasted_iota(jnp.int32, (SLAB, 128), 1) < 64

    def arranged(source):
        tiles = [source[:, 128 * i : 128 * i + 128] for i in range(5)]
        turned = [pltpu.roll(tiles[i], 64, 1) for i in (2, 3, 4)]
        even = (tiles[1], tiles[2], jnp.where(left, tiles[2], tiles[0]))
        odd = (
            jnp.where(left, turned[0], turned[1]),
            jnp.where(left, turned[1], turned[2]),
            jnp.where(left, turned[1], turned[0]),
        )
        blocks = {}
        for k in range(3):
            down = [jnp.where(band == 0, 0.0, pltpu.roll(x[k], 1, 0)) for x in (even, odd)]
            up = [jnp.where(band == SLAB - 1, 0.0, pltpu.roll(x[k], SLAB - 1, 0)) for x in (even, odd)]
            for a, both in enumerate((down, [even[k], odd[k]], up)):
                blocks[a, k] = jnp.concatenate(both, axis=0).astype(BF16)
        return blocks

    def where(frame, group):
        return pl.ds(pl.multiple_of(frame * HALF + group * 16, 16), 16)

    def lanes_of(ref, frame, group):
        return ref[frame, :, pl.ds(pl.multiple_of(group * 384, 128), 640)].astype(F32)

    loads[3].wait()

    def own_rows(group, carry):
        own0, own1 = arranged(lanes_of(own, 0, group)), arranged(lanes_of(own, 1, group))
        for a, k in own0:
            rows[0, a, k, where(0, group)] = own0[a, k]
            rows[0, a, k, where(1, group)] = own1[a, k]
            rows[1, a, k, where(1, group)] = jnp.where(room1 >= 1, own0[a, k], own1[a, k])
        return carry

    lax.fori_loop(0, GROUPS, own_rows, 0, unroll=10)

    def left_side(t, reads, lo, count):
        return jnp.concatenate([rows[t, a, k, lo : lo + count] for a in range(3) for k in reads], axis=1)

    for start, end, reads in SPANS:
        for at in range(0, 2 * HALF, STEP):
            centre = jnp.concatenate([rows[0, 1, k, at : at + STEP] for k in reads], axis=1)
            feats[at : at + STEP, start:end] = mix(centre, wide_stem[:, start:end]).astype(BF16)
        for at in range(0, HALF, STEP):
            acc[at : at + STEP, start:end] = mix(left_side(0, reads, at, STEP), wide[0:768, start:end])
        for at in range(HALF, 2 * HALF, STEP):
            both = jnp.concatenate([left_side(0, reads, at, STEP), left_side(1, reads, at, STEP)], axis=1)
            acc[at : at + STEP, start:end] = mix(both, wide[0:1536, start:end])

    def halo_rows(halo_frame, group, carry):
        new = arranged(lanes_of(halo, halo_frame, group))
        for a, k in new:
            if halo_frame == 1:
                rows[1, a, k, where(0, group)] = jnp.where(room0 >= 1, new[a, k], rows[0, a, k, where(0, group)])
                rows[2, a, k, where(1, group)] = jnp.where(room1 >= 2, new[a, k], rows[1, a, k, where(1, group)])
            else:
                rows[2, a, k, where(0, group)] = jnp.where(room0 >= 2, new[a, k], rows[1, a, k, where(0, group)])
        return carry

    def finish(frame, lo, count):
        at = frame * HALF + lo
        for start, end, reads in SPANS:
            value = acc[at : at + count, start:end] + mix(left_side(2, reads, at, count), wide[1536:, start:end])
            branch = (value * (0.5 * jnp.tanh(0.5 * value) + 0.5)).astype(BF16)
            result = (feats[at : at + count, start:end].astype(F32) + branch.astype(F32)).astype(BF16)
            for g in range(count // 8):
                to = (lo // 8 + g) * 768
                out[frame, :, to + start : to + end] = result[8 * g : 8 * g + 8]

    for send, (halo_frame, first_group, end_group) in zip(sends, pieces):
        @pl.when(me > 0)
        def _():
            send.wait_recv()

        number = end_group - first_group
        lax.fori_loop(
            first_group, end_group, functools.partial(halo_rows, halo_frame), 0, unroll=number if number <= 14 else 10
        )
        lo, count = 16 * first_group, 16 * number
        if halo_frame == 1:
            for start, end, reads in SPANS:
                acc[lo : lo + count, start:end] += mix(left_side(1, reads, lo, count), wide[768:1536, start:end])
            finish(1, lo, count)
        else:
            finish(0, lo, count)

    @pl.when(me < LAST)
    def _():
        for send in sends:
            send.wait_send()


def body(patches, clip_lengths, stem_weight, spatial_weight, temporal_weight):
    operands = (clip_lengths, patches, stem_weight, spatial_weight, temporal_weight)
    return pl.pallas_call(
        kernel,
        out_shape=pltpu.VMEM((2, SLAB, COLS * CH), BF16),
        in_specs=[pl.BlockSpec(memory_space=pltpu.HBM)] * 5,
        scratch_shapes=[
            pltpu.SMEM((16,), jnp.int32),
            pltpu.VMEM((2, SLAB, LANES + 256), BF16),
            pltpu.VMEM((2, SLAB, LANES + 256), BF16),
            pltpu.VMEM((PATCH, CH), BF16),
            pltpu.VMEM((3, 3, CH, CH), BF16),
            pltpu.VMEM((3, CH, CH), BF16),
            pltpu.VMEM((9 * PATCH, CH), F32),
            pltpu.VMEM((3, 4, 9 * PATCH, 128), BF16),
            pltpu.VMEM((4, PATCH, 128), BF16),
            pltpu.VMEM((9 * 256, 256 * TILES), BF16),
            pltpu.VMEM((256, 256 * TILES), BF16),
            pltpu.VMEM((3, 3, 3, 2 * HALF, 128), BF16),
            pltpu.VMEM((2 * HALF, 256 * TILES), F32),
            pltpu.VMEM((2 * HALF, 256 * TILES), BF16),
            pltpu.SemaphoreType.DMA((5,)),
            pltpu.SemaphoreType.DMA((CHUNKS,)),
            pltpu.SemaphoreType.DMA((CHUNKS,)),
        ],
        compiler_params=pltpu.CompilerParams(
            collective_id=0, has_side_effects=True, vmem_limit_bytes=44 << 20
        ),
        cost_estimate=pl.CostEstimate(flops=10_000_000_000, bytes_accessed=4_000_000, transcendentals=1_000_000),
    )(*[pltpu.with_memory_space_constraint(x, pltpu.HBM) for x in operands])


def solution(mesh):
    return jax.shard_map(
        body,
        mesh=mesh,
        in_specs=(P(("clip", "row"), None, None), P(), P(), P(), P()),
        out_specs=P(("clip", "row"), None, None),
        check_vma=False,
    )
```

```python
import functools

import jax
import jax.numpy as jnp
from jax import lax
from jax.experimental import pallas as pl
from jax.experimental.pallas import tpu as pltpu
from jax.sharding import PartitionSpec as P

MESH = pl.DeviceIdType.MESH
BF16, F32 = jnp.bfloat16, jnp.float32

CH = 192
PATCH = 48
COLS = 320
SLAB = 8
LANES = COLS * PATCH
GROUPS = 40
TILES = 3
HALF = 640
CUTS1 = (0, 20, 40)
CUTS0 = (0, 14, 28, 40)
DIRECT = 1
CHUNKS = len(CUTS1) + len(CUTS0) - 2
LAST = 127
MOST = 14
STEP = 160
SPANS = ((0, 256, (0, 2)), (256, 768, (0, 1)))


def lane_block(tile, block):
    return block - 16 if tile == 0 and block >= 12 else block


def mix(a, b):
    return jnp.dot(a, b, preferred_element_type=F32)


def spread(values, keep, kind):
    rows = values.shape[0]
    wide = jnp.concatenate([values, jnp.zeros((rows, 64), F32)], axis=1)
    back = pltpu.roll(wide, 192, 1)
    ahead = pltpu.roll(wide, 64, 1)
    keep[kind + (0,)] = wide[:, :128].astype(BF16)
    keep[kind + (1,)] = back[:, :128].astype(BF16)
    keep[kind + (2,)] = wide[:, 128:].astype(BF16)
    keep[kind + (3,)] = ahead[:, :128].astype(BF16)


def block_of(small, tile, half, block, base, first, count):
    lanes = 2 * tile + half
    pixel = 2 * (lanes // 3)
    place = lane_block(tile, block)

    def take(pix, arrangement):
        row = place - 3 * (pix + first)
        if 0 <= row < count:
            return small(arrangement, base + 16 * row)
        return None

    if lanes % 3 == 0:
        parts = [take(pixel, 0)]
    elif lanes % 3 == 2:
        parts = [take(pixel + 1, 1)]
    else:
        parts = [take(pixel, 2), take(pixel + 1, 3)]
    parts = [part for part in parts if part is not None]
    if not parts:
        return None
    return parts[0] if len(parts) == 1 else parts[0] + parts[1]


def kernel(
    lengths_hbm, patches, stem_hbm, spatial_hbm, temporal_hbm, out,
    lengths, own, halo, stem, spatial, temporal, folded, small, small_stem, wide, wide_stem, rows, acc, feats,
    load_sem, send_sem, recv_sem,
):
    clip, row = lax.axis_index("clip"), lax.axis_index("row")
    me = clip * 8 + row

    def place(device):
        return (device // 8, lax.rem(device, 8))

    loads = [
        pltpu.make_async_copy(spatial_hbm, spatial, load_sem.at[0]),
        pltpu.make_async_copy(stem_hbm, stem, load_sem.at[1]),
        pltpu.make_async_copy(temporal_hbm, temporal, load_sem.at[2]),
        pltpu.make_async_copy(patches, own.at[:, :, pl.ds(128, LANES)], load_sem.at[3]),
        pltpu.make_async_copy(lengths_hbm, lengths, load_sem.at[4]),
    ]
    barrier = pltpu.get_barrier_semaphore()

    @pl.when(me > 0)
    def _():
        pl.semaphore_signal(barrier, inc=1, device_id=place(me - 1), device_id_type=MESH)

    sends, pieces = [], []
    for frame, cuts in ((1, CUTS1), (0, CUTS0)):
        edges = [0] + [384 * cut + 128 for cut in cuts[1:-1]] + [LANES]
        for c in range(len(cuts) - 1):
            lo, hi = edges[c], edges[c + 1]
            pieces.append((frame, cuts[c], cuts[c + 1]))
            source, begin = (patches, 0) if len(sends) < DIRECT else (own, 128)
            sends.append(
                pltpu.make_async_remote_copy(
                    source.at[frame, :, pl.ds(begin + lo, hi - lo)],
                    halo.at[frame, :, pl.ds(128 + lo, hi - lo)],
                    send_sem.at[len(sends)],
                    recv_sem.at[len(sends)],
                    device_id=place(jnp.minimum(me + 1, LAST)),
                    device_id_type=MESH,
                )
            )

    def start_sends():
        pl.semaphore_wait(barrier, 1)
        for send in sends[:DIRECT]:
            send.start()

    def start_others():
        loads[3].wait()
        for send in sends[DIRECT:]:
            send.start()

    ends = row >= 6
    pl.when(jnp.logical_and(ends, me < LAST))(start_sends)
    for load in loads[::-1]:
        load.start()

    pl.when(jnp.logical_and(ends, me < LAST))(start_others)
    loads[4].wait()
    first, total = jnp.int32(0), jnp.int32(0)
    first_next = jnp.int32(0)
    for k in range(16):
        first = jnp.where(total <= 2 * me, total, first)
        first_next = jnp.where(total <= 2 * me + 1, total, first_next)
        total = total + lengths[k]
    room0 = 2 * me - first
    room1 = 2 * me + 1 - first_next

    side = jnp.zeros((2, SLAB, 128), BF16)
    for ref in (own, halo):
        ref[:, :, :128] = side
        ref[:, :, LANES + 128:] = side

    def clear(tap, carry):
        for tile in range(TILES):
            for half in range(2):
                for block in range(16):
                    if block_of(lambda arrangement, row: 0, tile, half, block, 0, -1, 9) is None:
                        to = pl.ds(pl.multiple_of(tap * 256 + 16 * block, 16), 16)
                        lanes = 256 * tile + 128 * half
                        wide[to, lanes : lanes + 128] = jnp.zeros((16, 128), BF16)
        return carry

    lax.fori_loop(0, 9, clear, 0)
    loads[0].wait()
    loads[1].wait()
    for tap in range(9):
        folded[48 * tap : 48 * tap + 48] = mix(stem[...], spatial[tap // 3, tap % 3])
    spread(stem[...].astype(F32), small_stem, ())
    loads[2].wait()
    upper = folded[...].astype(BF16)
    lower = (folded[...] - upper.astype(F32)).astype(BF16)
    for t in range(3):
        spread(mix(upper, temporal[t]) + mix(lower, temporal[t]), small, (t,))

    def widen(tap, carry):
        t, a = tap // 3, lax.rem(tap, 3)
        base = a * 144
        for tile in range(TILES):
            for half in range(2):
                for block in range(16):
                    value = block_of(
                        lambda arrangement, row: small[t, arrangement, pl.ds(pl.multiple_of(row, 16), 16)],
                        tile, half, block, base, -1, 9,
                    )
                    to = pl.ds(pl.multiple_of(tap * 256 + 16 * block, 16), 16)
                    lanes = 256 * tile + 128 * half
                    if value is not None:
                        wide[to, lanes : lanes + 128] = value
        return carry

    lax.fori_loop(0, 9, widen, 0)
    for tile in range(TILES):
        for half in range(2):
            for block in range(16):
                value = block_of(
                    lambda arrangement, row: small_stem[arrangement, row : row + 16], tile, half, block, 0, 0, 3
                )
                lanes = 256 * tile + 128 * half
                wide_stem[16 * block : 16 * block + 16, lanes : lanes + 128] = (
                    jnp.zeros((16, 128), BF16) if value is None else value
                )

    @pl.when(jnp.logical_not(ends))
    def _():
        start_sends()
        start_others()

    band = lax.broadcasted_iota(jnp.int32, (SLAB, 128), 0)
    left = lax.broadcasted_iota(jnp.int32, (SLAB, 128), 1) < 64

    def arranged(source):
        tiles = [source[:, 128 * i : 128 * i + 128] for i in range(5)]
        turned = [pltpu.roll(tiles[i], 64, 1) for i in (2, 3, 4)]
        even = (tiles[1], tiles[2], jnp.where(left, tiles[2], tiles[0]))
        odd = (
            jnp.where(left, turned[0], turned[1]),
            jnp.where(left, turned[1], turned[2]),
            jnp.where(left, turned[1], turned[0]),
        )
        blocks = {}
        for k in range(3):
            down = [jnp.where(band == 0, 0.0, pltpu.roll(x[k], 1, 0)) for x in (even, odd)]
            up = [jnp.where(band == SLAB - 1, 0.0, pltpu.roll(x[k], SLAB - 1, 0)) for x in (even, odd)]
            for a, both in enumerate((down, [even[k], odd[k]], up)):
                blocks[a, k] = jnp.concatenate(both, axis=0).astype(BF16)
        return blocks

    def where(frame, group):
        return pl.ds(pl.multiple_of(frame * HALF + group * 16, 16), 16)

    def lanes_of(ref, frame, group):
        return ref[frame, :, pl.ds(pl.multiple_of(group * 384, 128), 640)].astype(F32)

    pl.when(me == LAST)(loads[3].wait)

    def own_rows(group, carry):
        own0, own1 = arranged(lanes_of(own, 0, group)), arranged(lanes_of(own, 1, group))
        for a, k in own0:
            rows[0, a, k, where(0, group)] = own0[a, k]
            rows[0, a, k, where(1, group)] = own1[a, k]
            rows[1, a, k, where(1, group)] = jnp.where(room1 >= 1, own0[a, k], own1[a, k])
        return carry

    lax.fori_loop(0, GROUPS, own_rows, 0, unroll=10)

    def left_side(t, reads, lo, count):
        return jnp.concatenate([rows[t, a, k, lo : lo + count] for a in range(3) for k in reads], axis=1)

    for start, end, reads in SPANS:
        for at in range(0, 2 * HALF, STEP):
            centre = jnp.concatenate([rows[0, 1, k, at : at + STEP] for k in reads], axis=1)
            feats[at : at + STEP, start:end] = mix(centre, wide_stem[:, start:end]).astype(BF16)
        for at in range(0, HALF, STEP):
            acc[at : at + STEP, start:end] = mix(left_side(0, reads, at, STEP), wide[0:768, start:end])
        for at in range(HALF, 2 * HALF, STEP):
            both = jnp.concatenate([left_side(0, reads, at, STEP), left_side(1, reads, at, STEP)], axis=1)
            acc[at : at + STEP, start:end] = mix(both, wide[0:1536, start:end])

    def halo_rows(halo_frame, group, carry):
        new = arranged(lanes_of(halo, halo_frame, group))
        for a, k in new:
            if halo_frame == 1:
                rows[1, a, k, where(0, group)] = jnp.where(room0 >= 1, new[a, k], rows[0, a, k, where(0, group)])
                rows[2, a, k, where(1, group)] = jnp.where(room1 >= 2, new[a, k], rows[1, a, k, where(1, group)])
            else:
                rows[2, a, k, where(0, group)] = jnp.where(room0 >= 2, new[a, k], rows[1, a, k, where(0, group)])
        return carry

    def finish(frame, lo, count):
        at = frame * HALF + lo
        for start, end, reads in SPANS:
            value = acc[at : at + count, start:end] + mix(left_side(2, reads, at, count), wide[1536:, start:end])
            branch = (value * (0.5 * jnp.tanh(0.5 * value) + 0.5)).astype(BF16)
            result = (feats[at : at + count, start:end].astype(F32) + branch.astype(F32)).astype(BF16)
            for g in range(count // 8):
                to = (lo // 8 + g) * 768
                out[frame, :, to + start : to + end] = result[8 * g : 8 * g + 8]

    for send, (halo_frame, first_group, end_group) in zip(sends, pieces):
        @pl.when(me > 0)
        def _():
            send.wait_recv()

        parts = -((first_group - end_group) // MOST)
        marks = [first_group + (end_group - first_group) * i // parts for i in range(parts + 1)]
        for low, high in zip(marks[:-1], marks[1:]):
            lax.fori_loop(low, high, functools.partial(halo_rows, halo_frame), 0, unroll=high - low)
            lo, count = 16 * low, 16 * (high - low)
            if halo_frame == 1:
                for start, end, reads in SPANS:
                    acc[lo : lo + count, start:end] += mix(left_side(1, reads, lo, count), wide[768:1536, start:end])
            finish(halo_frame, lo, count)

    @pl.when(me < LAST)
    def _():
        for send in sends:
            send.wait_send()


def body(patches, clip_lengths, stem_weight, spatial_weight, temporal_weight):
    operands = (clip_lengths, patches, stem_weight, spatial_weight, temporal_weight)
    return pl.pallas_call(
        kernel,
        out_shape=pltpu.VMEM((2, SLAB, COLS * CH), BF16),
        in_specs=[pl.BlockSpec(memory_space=pltpu.HBM)] * 5,
        scratch_shapes=[
            pltpu.SMEM((16,), jnp.int32),
            pltpu.VMEM((2, SLAB, LANES + 256), BF16),
            pltpu.VMEM((2, SLAB, LANES + 256), BF16),
            pltpu.VMEM((PATCH, CH), BF16),
            pltpu.VMEM((3, 3, CH, CH), BF16),
            pltpu.VMEM((3, CH, CH), BF16),
            pltpu.VMEM((9 * PATCH, CH), F32),
            pltpu.VMEM((3, 4, 9 * PATCH, 128), BF16),
            pltpu.VMEM((4, PATCH, 128), BF16),
            pltpu.VMEM((9 * 256, 256 * TILES), BF16),
            pltpu.VMEM((256, 256 * TILES), BF16),
            pltpu.VMEM((3, 3, 3, 2 * HALF, 128), BF16),
            pltpu.VMEM((2 * HALF, 256 * TILES), F32),
            pltpu.VMEM((2 * HALF, 256 * TILES), BF16),
            pltpu.SemaphoreType.DMA((5,)),
            pltpu.SemaphoreType.DMA((CHUNKS,)),
            pltpu.SemaphoreType.DMA((CHUNKS,)),
        ],
        compiler_params=pltpu.CompilerParams(
            collective_id=0, has_side_effects=True, vmem_limit_bytes=44 << 20
        ),
        cost_estimate=pl.CostEstimate(flops=10_000_000_000, bytes_accessed=4_000_000, transcendentals=1_000_000),
    )(*[pltpu.with_memory_space_constraint(x, pltpu.HBM) for x in operands])


def solution(mesh):
    return jax.shard_map(
        body,
        mesh=mesh,
        in_specs=(P(("clip", "row"), None, None), P(), P(), P(), P()),
        out_specs=P(("clip", "row"), None, None),
        check_vma=False,
    )
```
